512 devices in a mesh: ep: 16 (over y, core), etp: 32 (over z, x).
Axes of the slice: x: 4, y: 8, z: 8, core: 2. Of those that a mesh axis runs over, the one named last changes fastest.
Arguments:
- tokens: bfloat16 [2048, 3072], P('ep', 'etp'), may hold values from -6 to 6
- routes: int32 [2048, 4], P('ep'), may hold values from 0 to 15, all different within a row; in each aligned block of 128 rows (0 to 127, 128 to 255, ...) at most 36 rows name the same one
- gate_fixed: int32 [2048, 4], P('ep'), may hold values from 3277 to 65535
- gate_weight: bfloat16 [16, 8192, 3072], P('ep', 'etp'), may hold values from -0.21875 to 0.21875
- up_weight: bfloat16 [16, 8192, 3072], P('ep', 'etp'), may hold values from -0.21875 to 0.21875
- down_weight: bfloat16 [16, 8192, 3072], P('ep', 'etp'), may hold values from -0.125 to 0.125
- cotangent: bfloat16 [2048, 3072], P('ep', 'etp'), may hold values from -6 to 6
Outputs:
- layer_output: bfloat16 [2048, 3072], P('ep', 'etp')
- grad_tokens: bfloat16 [2048, 3072], P('ep', 'etp')
The draws below stay inside these ranges and needn't reach their ends.
Inputs may be any that keep to these rules, and one draw needn't show every extreme that they name: `routes`: A row names 4 different experts. Among the 128 rows of one ep index no expert is named by more than 36 rows, and in every draw some expert is named by exactly 36 rows of some ep index.
All inputs are finite; a program needn't handle non-finite values.
Results may differ from the reference program's by a relative error of at most 0.02.
Values may be sent and summed in bfloat16 or wider, within the bound.
No kernel may reach another device: no remote copies, remote signals or barrier semaphores. Data moves between devices by JAX's collectives and lax.ppermute only.
A program may use at most 128 MiB of HBM per device.

```python
import math
import jax
import jax.numpy as jnp
import numpy as np
from jax import lax

D = 3072
FF = 8192
TOP = 4
TOK_DEV = 128
EXPERTS = 16
TOKENS = 2048
FF_DEV = 256
CAP = 36
N_ETP = 32


def plant(result, stream_key, least, largest):
    extent = result.shape
    place = [jax.random.randint(jax.random.fold_in(stream_key, axis), (), 0, extent[axis]) for axis in range(len(extent))]
    result = result.at[tuple(place)].set(least)
    longest = extent.index(max(extent))
    place[longest] = (place[longest] + 1) % extent[longest]
    return result.at[tuple(place)].set(largest)


def with_spikes(values, key, source, target, parts, factor):
    owner, partner = [(jnp.arange(values.shape[position]) // (values.shape[position] // parts)).reshape([-1 if axis == position else 1 for axis in range(values.ndim)]) for position in (source, target)]
    chosen = jax.random.permutation(key, parts)[partner]
    strong = (owner == chosen) | (owner == (partner + parts // 2) % parts)
    return jnp.where(strong, factor * values, values)


def shard_levels(rng, extent, split, smallest, largest):
    def one(position, blocks):
        heights = jax.random.uniform(jax.random.fold_in(jax.random.fold_in(rng, 6), position), (blocks,), jnp.float32, smallest / len(split), largest / len(split))
        return jnp.repeat(jnp.exp(heights), extent[position] // blocks).reshape((-1,) + (1,) * (len(extent) - position - 1))

    factor_of = one(*split[0])
    for cut in split[1:]:
        factor_of = factor_of * one(*cut)
    return factor_of


def shared_out(key, own, number, rows, amount, top, most, skew):
    order = jax.random.permutation(key, amount)
    packed, ordinary = load_shares(amount, rows * top, most, skew, True), load_shares(amount, rows * top, most, skew, False)
    places = jnp.arange(amount)

    def named(sizes, offset_by):
        used = int((sizes > 0).sum())
        fixed = max(1, used // 4)
        moved = fixed + (places - fixed + offset_by * (used - fixed)) % max(1, amount - fixed)
        return jnp.zeros((amount,), jnp.int32).at[order[jnp.where(places < fixed, places, moved)]].set(jnp.asarray(sizes, jnp.int32))

    sizes = jnp.where(number % 4 == 0, named(packed, number // 4), named(ordinary, number - number // 4 - 1))
    mixed = jax.random.permutation(jax.random.fold_in(own, 3), amount)
    donor, sink = mixed[0:amount // 2 * 2:2], mixed[1:amount // 2 * 2:2]
    slack = jnp.minimum(sizes[donor] - 1, most - sizes[sink]) // 2
    slack = jnp.where((donor == order[0]) | (sink == order[0]) | (sizes[sink] == 0), 0, jnp.maximum(slack, 0))
    moved = jax.random.randint(jax.random.fold_in(own, 4), (amount // 2,), 0, 1 << 20) % (slack + 1)
    sizes = sizes.at[donor].add(-moved).at[sink].add(moved)
    items = jnp.searchsorted(jnp.cumsum(sizes), jnp.arange(rows * top), side="right").astype(jnp.int32)
    listing = items.reshape(top, rows).T
    listing = listing[jax.random.permutation(jax.random.fold_in(own, 1), rows)]
    offset_by = jax.random.randint(jax.random.fold_in(own, 2), (rows, 1), 0, top)
    return jnp.take_along_axis(listing, (jnp.arange(top)[None, :] + offset_by) % top, axis=1)


def load_shares(number_of, total, most, lean, full):
    weights = [(1 << 20) // math.isqrt(standing ** lean) + 1 for standing in range(1, number_of + 1)]
    largest = most if full else min(most, max(-(-total // number_of), total * weights[0] // sum(weights)))
    least = 1 if total - largest >= number_of - 1 else 0
    holding, spare = [largest] + [least] * (number_of - 1), total - largest - least * (number_of - 1)
    while spare > 0:
        free = [i for i in range(1, number_of) if holding[i] < largest] or [i for i in range(1, number_of) if holding[i] < most]
        mass, left = sum([weights[i] for i in free]), spare
        for i in free:
            more = min(most - holding[i], max(1, left * weights[i] // mass), spare)
            holding[i] = holding[i] + more
            spare = spare - more
    return np.array(holding)


def centred(rng, shape, deviation, bound, split=(), held_as=jnp.bfloat16):
    loudness = shard_levels(rng, shape, split, -0.22, 0.18) if split else 1.0
    drawn = jax.random.normal(rng, shape, jnp.float32) * deviation * loudness
    return jnp.minimum(jnp.maximum(drawn, -bound), bound).astype(held_as)


def noise_with(rng, dims, width, bound, split, heavy, kind=jnp.bfloat16):
    values = width * jax.random.normal(rng, dims, jnp.float32)
    if split:
        values = values * shard_levels(rng, dims, split, -0.22, 0.18)
    return jnp.clip(with_spikes(values, jax.random.fold_in(rng, 3), *heavy), -bound, bound).astype(kind)


def setup_inputs(seed: int = 0) -> dict:
    key_list = jax.random.split(jax.random.key(seed), 8)
    tokens = centred(key_list[0], (TOKENS, D), 1.0, 6.0, ((0, 16), (1, 32)))
    routes_keys = jax.random.split(jax.random.fold_in(key_list[1], 1), TOKENS // TOK_DEV)
    routes_turns = jax.random.permutation(jax.random.fold_in(key_list[1], 3), TOKENS // TOK_DEV)
    routes = jax.vmap(lambda own, number: shared_out(jax.random.fold_in(key_list[1], 2), own, number, TOK_DEV, EXPERTS, TOP, CAP, 2))(routes_keys, routes_turns).reshape((TOKENS, TOP))
    gate_fixed = plant(jax.random.randint(key_list[2], (TOKENS, TOP), 3277, 65536), jax.random.fold_in(key_list[2], 1), 3277, 65535).astype(jnp.int32)
    gate_weight = noise_with(key_list[3], (EXPERTS, FF, D), D ** -0.5, 0.21875, ((0, 16), (1, 32)), (1, 2, 32, 2.75))
    up_weight = noise_with(key_list[4], (EXPERTS, FF, D), D ** -0.5, 0.21875, ((0, 16), (1, 32)), (1, 2, 32, 2.75))
    down_weight = noise_with(key_list[5], (EXPERTS, FF, D), FF ** -0.5, 0.125, ((0, 16), (1, 32)), (1, 2, 32, 2.75))
    cotangent = centred(key_list[6], (TOKENS, D), 1.0, 6.0, ((0, 16), (1, 32)))
    return dict(tokens=tokens, routes=routes, gate_fixed=gate_fixed, gate_weight=gate_weight, up_weight=up_weight, down_weight=down_weight, cotangent=cotangent)


fixed_point = 65536.0


def silu_parts(pre_gate):
    sigmoid_value = jax.nn.sigmoid(pre_gate)
    activated = pre_gate * sigmoid_value
    derivative = sigmoid_value * (1.0 + pre_gate * (1.0 - sigmoid_value))
    return activated, derivative


def rounded(values):
    return lax.optimization_barrier(values.astype(jnp.bfloat16))


def take_rows(source, indices):
    return jax.vmap(lambda matrix, chosen: jnp.take(matrix, chosen, axis=0))(source, indices)


def placement(routes, blocks):
    entries = TOK_DEV * TOP
    flattened = routes.reshape(blocks, entries)
    expert_ids = jnp.arange(EXPERTS, dtype=jnp.int32)
    onehot = (flattened[:, :, None] == expert_ids[None, None, :]).astype(jnp.int32)
    earlier = jnp.cumsum(onehot, axis=1) - onehot
    slot_index = jnp.sum(earlier * onehot, axis=2).astype(jnp.int32)
    target = (flattened * CAP + slot_index).astype(jnp.int32)
    block_ids = jnp.arange(blocks, dtype=jnp.int32)[:, None]
    numbers = jnp.broadcast_to(jnp.arange(entries, dtype=jnp.int32)[None, :], (blocks, entries))
    slot_table = jnp.full((blocks, EXPERTS * CAP), entries, jnp.int32).at[block_ids, target].set(numbers)
    return target, slot_table


def reference(tokens, routes, gate_fixed, gate_weight, up_weight, down_weight, cotangent):
    blocks = TOKENS // TOK_DEV
    entries = TOK_DEV * TOP
    target, slot_table = placement(routes, blocks)
    gate_value = gate_fixed.astype(jnp.float32) / fixed_point
    owners = (slot_table // TOP).astype(jnp.int32)
    zero_row = jnp.zeros((blocks, 1, D), tokens.dtype)
    token_rows = take_rows(jnp.concatenate([tokens.reshape(blocks, TOK_DEV, D), zero_row], axis=1), owners)
    cot_rows = take_rows(jnp.concatenate([cotangent.reshape(blocks, TOK_DEV, D), zero_row.astype(cotangent.dtype)], axis=1), owners)
    gate_pad = jnp.concatenate([gate_value.reshape(blocks, entries), jnp.zeros((blocks, 1), jnp.float32)], axis=1)
    slot_gate = jax.vmap(lambda row_gates, chosen: jnp.take(row_gates, chosen))(gate_pad, slot_table)
    grad_rows = rounded(cot_rows.astype(jnp.float32) * slot_gate[:, :, None])

    def to_experts(buffer):
        return buffer.reshape(blocks, EXPERTS, CAP, D).transpose(1, 0, 2, 3).reshape(EXPERTS, blocks * CAP, D)

    def to_sources(buffer):
        arranged = buffer.reshape(EXPERTS, blocks, CAP, D).transpose(1, 0, 2, 3).reshape(blocks, EXPERTS * CAP, D)
        return take_rows(arranged, target).reshape(TOKENS, TOP, D)

    expert_inputs = to_experts(token_rows).astype(jnp.float32)
    expert_grads = to_experts(grad_rows).astype(jnp.float32)

    def one_block(totals, block_index):
        out_total, grad_total = totals
        offset = (block_index * FF_DEV).astype(jnp.int32)
        gate_part = lax.dynamic_slice_in_dim(gate_weight, offset, FF_DEV, 1).astype(jnp.float32)
        up_part = lax.dynamic_slice_in_dim(up_weight, offset, FF_DEV, 1).astype(jnp.float32)
        down_part = lax.dynamic_slice_in_dim(down_weight, offset, FF_DEV, 1).astype(jnp.float32)
        pre_gate = jnp.einsum("erd,efd->erf", expert_inputs, gate_part)
        pre_up = jnp.einsum("erd,efd->erf", expert_inputs, up_part)
        activated, derivative = silu_parts(pre_gate)
        hidden = rounded(activated * pre_up).astype(jnp.float32)
        part_out = rounded(jnp.einsum("erf,efd->erd", hidden, down_part))
        mixed_part = rounded(jnp.sum(to_sources(part_out).astype(jnp.float32) * gate_value[:, :, None], axis=1))
        grad_hidden = jnp.einsum("erd,efd->erf", expert_grads, down_part)
        grad_gate = rounded(grad_hidden * pre_up * derivative).astype(jnp.float32)
        grad_up = rounded(grad_hidden * activated).astype(jnp.float32)
        part_in = rounded(jnp.einsum("erf,efd->erd", grad_gate, gate_part) + jnp.einsum("erf,efd->erd", grad_up, up_part))
        grad_part = rounded(jnp.sum(to_sources(part_in).astype(jnp.float32), axis=1))
        new_totals = (out_total + mixed_part.astype(jnp.float32), grad_total + grad_part.astype(jnp.float32))
        return new_totals, None

    start_totals = (jnp.zeros((TOKENS, D), jnp.float32), jnp.zeros((TOKENS, D), jnp.float32))
    final_totals, unused = lax.scan(one_block, start_totals, jnp.arange(N_ETP, dtype=jnp.int32))
    layer_output = final_totals[0].astype(jnp.bfloat16)
    grad_tokens = final_totals[1].astype(jnp.bfloat16)
    return layer_output, grad_tokens
```

```python
import functools

import jax
import jax.numpy as jnp
from jax import lax
from jax.experimental import pallas as pl
from jax.experimental.pallas import tpu as pltpu
from jax.sharding import Mesh
from jax.sharding import PartitionSpec as P

EXPERTS = 16
CAP = 36
TOKENS_HERE = 128
FEATURES = 96
ROWS = EXPERTS * CAP
BOTH = 2 * ROWS
HIDDEN = 256
MAIN = 512
TAIL = ROWS - MAIN
EP = ("y", "c")
NT = (((1,), (1,)), ((), ()))
TN = (((0,), (0,)), ((), ()))


def f32_dot(a, b, dims):
    return lax.dot_general(a, b, dims, preferred_element_type=jnp.float32)


def slots(routes, gate_fixed):
    named = []
    gates = []
    for e in range(EXPERTS):
        hit = routes == e
        named.append(jnp.sum(hit.astype(jnp.float32), axis=0, keepdims=True))
        gates.append(jnp.sum(jnp.where(hit, gate_fixed, 0).astype(jnp.float32), axis=0, keepdims=True))
    member = jnp.concatenate(named, axis=0)
    before = lax.broadcasted_iota(jnp.int32, (TOKENS_HERE, TOKENS_HERE), 0)
    after = lax.broadcasted_iota(jnp.int32, (TOKENS_HERE, TOKENS_HERE), 1)
    earlier = (before < after).astype(jnp.bfloat16)
    rank = jnp.dot(member.astype(jnp.bfloat16), earlier, preferred_element_type=jnp.float32)
    rank = jnp.where(member > 0.0, rank, -1.0)
    slot = lax.broadcasted_iota(jnp.int32, (2 * CAP, TOKENS_HERE), 0)
    slot = jnp.where(slot >= CAP, slot - CAP, slot).astype(jnp.float32)
    onehot = [(rank[e : e + 1] == slot).astype(jnp.float32) for e in range(EXPERTS)]
    return onehot, gates


def row_of_slot(shape, axis):
    index = lax.broadcasted_iota(jnp.int32, shape, axis)
    return index - (index // (2 * CAP)) * (2 * CAP)


def dispatch_body(routes_ref, gate_ref, tokens_ref, cot_ref, out_ref):
    onehot, gates = slots(routes_ref[...], gate_ref[...])
    scaled = [jnp.sum(onehot[e] * gates[e], axis=1, keepdims=True) for e in range(EXPERTS)]
    scale = jnp.concatenate(scaled, axis=0) * (1.0 / 65536.0)
    chosen = jnp.concatenate(onehot, axis=0).astype(jnp.bfloat16)
    from_tokens = f32_dot(chosen, tokens_ref[...], NT)
    from_cot = f32_dot(chosen, cot_ref[...], NT) * scale
    is_token = row_of_slot((BOTH, FEATURES), 0) < CAP
    out_ref[...] = jnp.where(is_token, from_tokens, from_cot).astype(jnp.bfloat16)


def column_of(row):
    source = row // (2 * CAP)
    within = row - source * (2 * CAP)
    is_cot = (within >= CAP).astype(jnp.int32)
    number = source * CAP + within - is_cot * CAP
    return jnp.where(number < MAIN, number + MAIN * is_cot, number + MAIN + TAIL * is_cot)


def placing():
    row = lax.broadcasted_iota(jnp.int32, (BOTH, 1), 0)
    column = lax.broadcasted_iota(jnp.int32, (BOTH, BOTH), 1)
    return (column_of(row) == column).astype(jnp.bfloat16)


def to_columns_body(rows_ref, out_ref):
    out_ref[...] = f32_dot(rows_ref[...], placing(), TN).astype(jnp.bfloat16)


def to_rows_body(columns_ref, out_ref):
    out_ref[...] = f32_dot(placing(), columns_ref[...], NT).astype(jnp.bfloat16)


def combine_body(routes_ref, gate_ref, rows_ref, out_ref, grad_ref):
    onehot, gates = slots(routes_ref[...], gate_ref[...])
    high, low = [], []
    for e in range(EXPERTS):
        top = jnp.floor(gates[e] * (1.0 / 256.0))
        high.append(onehot[e] * top)
        low.append(onehot[e] * (gates[e] - 256.0 * top))
    is_token = row_of_slot((BOTH, TOKENS_HERE), 0) < CAP
    high = jnp.where(is_token, jnp.concatenate(high, axis=0), 0.0).astype(jnp.bfloat16)
    low = jnp.where(is_token, jnp.concatenate(low, axis=0), 0.0).astype(jnp.bfloat16)
    whole = jnp.where(is_token, 0.0, jnp.concatenate(onehot, axis=0)).astype(jnp.bfloat16)
    rows = rows_ref[...]
    mixed = f32_dot(rows, high, TN) * (1.0 / 256.0) + f32_dot(rows, low, TN) * (1.0 / 65536.0)
    out_ref[...] = mixed.astype(jnp.bfloat16)
    grad_ref[...] = f32_dot(rows, whole, TN).astype(jnp.bfloat16)


def expert_body(x_ref, gate_ref, up_ref, down_ref, y_ref):
    gate, up, down = gate_ref[0], up_ref[0], down_ref[0]
    tail_columns = pl.ds(2 * MAIN, 2 * TAIL)
    nn = (((1,), (0,)), ((), ()))

    def middle(pre_gate, pre_up, grad_hidden):
        sig = jax.nn.sigmoid(pre_gate)
        activated = pre_gate * sig
        derivative = sig * (1.0 + pre_gate * (1.0 - sig))
        hidden = activated * pre_up
        grad_gate = grad_hidden * pre_up * derivative
        grad_up = grad_hidden * activated
        return hidden, grad_gate, grad_up

    x_main = x_ref[:, pl.ds(0, MAIN)]
    pre_gate = f32_dot(gate, x_main, nn)
    pre_up = f32_dot(up, x_main, nn)
    grad_hidden = f32_dot(down, x_ref[:, pl.ds(MAIN, MAIN)], nn)
    x_tail = x_ref[:, tail_columns]
    tail_gate = f32_dot(gate, x_tail, nn)
    tail_up = f32_dot(up, x_tail, nn)
    tail_grad = pltpu.roll(f32_dot(down, x_tail, nn), TAIL, 1)
    hidden, grad_gate, grad_up = middle(pre_gate, pre_up, grad_hidden)
    tail_hidden, tail_gg, tail_gu = middle(tail_gate, tail_up, tail_grad)
    first = lax.broadcasted_iota(jnp.int32, tail_hidden.shape, 1) < TAIL
    tail_hidden = jnp.where(first, tail_hidden, 0.0).astype(jnp.bfloat16)
    tail_gg = jnp.where(first, 0.0, pltpu.roll(tail_gg, TAIL, 1)).astype(jnp.bfloat16)
    tail_gu = jnp.where(first, 0.0, pltpu.roll(tail_gu, TAIL, 1)).astype(jnp.bfloat16)
    hidden = hidden.astype(jnp.bfloat16)
    grad_gate = grad_gate.astype(jnp.bfloat16)
    grad_up = grad_up.astype(jnp.bfloat16)

    block = 512

    @pl.loop(0, x_ref.shape[0] // block)
    def _(step):
        part = pl.ds(pl.multiple_of(step * block, block), block)
        g, u, d = gate_ref[0, :, part], up_ref[0, :, part], down_ref[0, :, part]
        y_ref[part, pl.ds(0, MAIN)] = f32_dot(d, hidden, TN).astype(jnp.bfloat16)
        y_ref[part, pl.ds(MAIN, MAIN)] = (f32_dot(g, grad_gate, TN) + f32_dot(u, grad_up, TN)).astype(jnp.bfloat16)
        tail = f32_dot(d, tail_hidden, TN) + f32_dot(g, tail_gg, TN) + f32_dot(u, tail_gu, TN)
        y_ref[part, tail_columns] = tail.astype(jnp.bfloat16)


def call(body, outs, *args, limit=None):
    return pl.pallas_call(
        body,
        out_shape=outs,
        compiler_params=pltpu.CompilerParams(vmem_limit_bytes=limit),
    )(*args)


def bf16(*shape):
    return jax.ShapeDtypeStruct(shape, jnp.bfloat16)


def shards(tokens, routes, gate_fixed, gate_weight, up_weight, down_weight, cotangent):
    routes_t, gate_t = routes.T, gate_fixed.T
    small = 24 * 2**20
    send = call(dispatch_body, bf16(BOTH, FEATURES), routes_t, gate_t, tokens.T, cotangent.T, limit=small)
    received = lax.all_to_all(send.reshape(EXPERTS, 2 * CAP, FEATURES), EP, 0, 0, tiled=True)
    columns = call(to_columns_body, bf16(FEATURES, BOTH), received.reshape(BOTH, FEATURES), limit=small)
    gathered = lax.all_gather(columns, ("z", "x"), axis=0, tiled=True)
    depth = gathered.shape[0]
    parts = call(expert_body, bf16(depth, BOTH), gathered, gate_weight, up_weight, down_weight, limit=48 * 2**20)
    parts = parts.reshape(8, 4, FEATURES, BOTH)
    summed = lax.psum_scatter(parts, "z", scatter_dimension=0, tiled=False)
    summed = lax.psum_scatter(summed, "x", scatter_dimension=0, tiled=False)
    back = call(to_rows_body, bf16(BOTH, FEATURES), summed, limit=small)
    home = lax.all_to_all(back.reshape(EXPERTS, 2 * CAP, FEATURES), EP, 0, 0, tiled=True)
    out, grad = call(
        combine_body,
        (bf16(FEATURES, TOKENS_HERE), bf16(FEATURES, TOKENS_HERE)),
        routes_t,
        gate_t,
        home.reshape(BOTH, FEATURES),
        limit=small,
    )
    return out.T, grad.T


def solution(mesh):
    fine = Mesh(mesh.devices.reshape(8, 2, 8, 4), ("y", "c", "z", "x"))
    ep, etp = EP, ("z", "x")
    placed = (P(ep, etp), P(ep, None), P(ep, None), P(ep, etp, None), P(ep, etp, None), P(ep, etp, None), P(ep, etp))
    return jax.shard_map(shards, mesh=fine, in_specs=placed, out_specs=(P(ep, etp), P(ep, etp)), check_vma=False)
```

```python
import jax
import jax.numpy as jnp
from jax import lax
from jax.experimental import pallas as pl
from jax.experimental.pallas import tpu as pltpu
from jax.sharding import Mesh
from jax.sharding import PartitionSpec as P

EXPERTS = 16
CAP = 36
TOKENS_HERE = 128
FEATURES = 96
ROWS = EXPERTS * CAP
MAIN = 512
TAIL = ROWS - MAIN
WIDE = MAIN + 2 * TAIL
NEAR = 384
PLANES = 8
STEP = 4 * FEATURES
DEPTH = PLANES * STEP
EP = ("y", "c")
ETP = ("z", "x")
RIGHT = [(0, 1), (1, 2), (2, 3), (3, 0)]
LEFT = [(1, 0), (2, 1), (3, 2), (0, 3)]
NT = (((1,), (1,)), ((), ()))
TN = (((0,), (0,)), ((), ()))
NN = (((1,), (0,)), ((), ()))


def f32_dot(a, b, dims):
    return lax.dot_general(a, b, dims, preferred_element_type=jnp.float32)


def slots(routes, gate_fixed):
    named = []
    gates = []
    for e in range(EXPERTS):
        hit = routes == e
        named.append(jnp.sum(hit.astype(jnp.float32), axis=0, keepdims=True))
        gates.append(jnp.sum(jnp.where(hit, gate_fixed, 0).astype(jnp.float32), axis=0, keepdims=True))
    member = jnp.concatenate(named, axis=0)
    before = lax.broadcasted_iota(jnp.int32, (TOKENS_HERE, TOKENS_HERE), 0)
    after = lax.broadcasted_iota(jnp.int32, (TOKENS_HERE, TOKENS_HERE), 1)
    earlier = (before < after).astype(jnp.bfloat16)
    rank = jnp.dot(member.astype(jnp.bfloat16), earlier, preferred_element_type=jnp.float32)
    rank = jnp.where(member > 0.0, rank, -1.0)
    slot = lax.broadcasted_iota(jnp.int32, (CAP, TOKENS_HERE), 0).astype(jnp.float32)
    onehot = [(rank[e : e + 1] == slot).astype(jnp.float32) for e in range(EXPERTS)]
    return onehot, gates


def dispatch_body(routes_ref, gate_ref, tokens_ref, cot_ref, out_ref):
    onehot, gates = slots(routes_ref[...], gate_ref[...])
    values = jnp.concatenate([tokens_ref[...], cot_ref[...]], axis=0)
    is_token = lax.broadcasted_iota(jnp.int32, (CAP, 2 * FEATURES), 1) < FEATURES
    for e in range(EXPERTS):
        scale = jnp.sum(onehot[e] * gates[e], axis=1, keepdims=True) * (1.0 / 65536.0)
        rows = f32_dot(onehot[e].astype(jnp.bfloat16), values, NT)
        out_ref[e] = (rows * jnp.where(is_token, 1.0, scale)).astype(jnp.bfloat16)


def place_of(source):
    slot = lax.broadcasted_iota(jnp.int32, (CAP, MAIN + 2 * TAIL), 0)
    number = lax.broadcasted_iota(jnp.int32, (CAP, MAIN + 2 * TAIL), 1)
    return (number == slot + source * CAP).astype(jnp.bfloat16)


def columns_body(rows_ref, first_ref, second_ref):
    total = jnp.zeros((2 * FEATURES, MAIN + 2 * TAIL), jnp.float32)
    for source in range(EXPERTS):
        total = total + f32_dot(rows_ref[source], place_of(source), TN)
    tokens, cotangent = total[:FEATURES], total[FEATURES:]
    first_ref[...] = tokens[:, :MAIN].astype(jnp.bfloat16)
    second_ref[:, pl.ds(0, MAIN)] = cotangent[:, :MAIN].astype(jnp.bfloat16)
    low = lax.broadcasted_iota(jnp.int32, (FEATURES, 2 * TAIL), 1) < TAIL
    tail = jnp.where(low, tokens[:, MAIN:], pltpu.roll(cotangent[:, MAIN:], TAIL, 1))
    second_ref[:, pl.ds(MAIN, 2 * TAIL)] = tail.astype(jnp.bfloat16)


def total_of(ref):
    total = ref[0].astype(jnp.float32)
    for k in range(1, ref.shape[0]):
        total = total + ref[k].astype(jnp.float32)
    return total


def rows_body(first_ref, second_ref, third_ref, out_ref):
    first = total_of(first_ref)
    second = jnp.concatenate([total_of(second_ref), total_of(third_ref)], axis=1)
    tail = second[:, MAIN:]
    low = lax.broadcasted_iota(jnp.int32, tail.shape, 1) < TAIL
    outs = jnp.concatenate([first, jnp.where(low, tail, 0.0)], axis=1)
    grads = jnp.concatenate([second[:, :MAIN], jnp.where(low, pltpu.roll(tail, TAIL, 1), 0.0)], axis=1)
    both = jnp.concatenate([outs, grads], axis=0).astype(jnp.bfloat16)
    for source in range(EXPERTS):
        out_ref[source] = f32_dot(place_of(source), both, NT).astype(jnp.bfloat16)


def combine_body(routes_ref, gate_ref, rows_ref, out_ref, grad_ref):
    onehot, gates = slots(routes_ref[...], gate_ref[...])
    total = jnp.zeros((2 * FEATURES, 3 * TOKENS_HERE), jnp.float32)
    for e in range(EXPERTS):
        high = jnp.floor(gates[e] * (1.0 / 256.0))
        low = gates[e] - 256.0 * high
        factors = jnp.concatenate([onehot[e] * high, onehot[e] * low, onehot[e]], axis=1).astype(jnp.bfloat16)
        total = total + f32_dot(rows_ref[e], factors, TN)
    by_high, by_low = total[:FEATURES, :TOKENS_HERE], total[:FEATURES, TOKENS_HERE : 2 * TOKENS_HERE]
    out_ref[...] = (by_high * (1.0 / 256.0) + by_low * (1.0 / 65536.0)).astype(jnp.bfloat16)
    grad_ref[...] = total[FEATURES:, 2 * TOKENS_HERE :].astype(jnp.bfloat16)


def activation(pre_gate, pre_up):
    sig = jax.nn.sigmoid(pre_gate)
    activated = pre_gate * sig
    derivative = sig * (1.0 + pre_gate * (1.0 - sig))
    return activated * pre_up, pre_up * derivative, activated


def start_all(copies):
    for copy in copies:
        copy.start()


def wait_all(copies):
    for copy in copies:
        copy.wait()


def forward_body(x_ref, gate_ref, up_ref, down_ref, y_ref, to_gate_ref, to_up_ref, x, gate, up, down, y, sems, out_sems):
    loads = [
        pltpu.make_async_copy(source, target, sems.at[number])
        for number, (source, target) in enumerate(((x_ref, x), (gate_ref, gate), (up_ref, up), (down_ref, down)))
    ]
    start_all(loads)
    wait_all(loads[:2])
    pre_gate = f32_dot(gate[0], x[...], NN)
    loads[2].wait()
    hidden, to_gate, to_up = activation(pre_gate, f32_dot(up[0], x[...], NN))
    to_gate_ref[...] = to_gate
    to_up_ref[...] = to_up
    hidden = hidden.astype(jnp.bfloat16)
    loads[3].wait()
    stores = []
    for step in range(PLANES):
        y[step] = f32_dot(down[0, :, pl.ds(step * STEP, STEP)], hidden, TN).astype(jnp.bfloat16)
        stores.append(pltpu.make_async_copy(y.at[step], y_ref.at[step], out_sems.at[step]))
        stores[-1].start()
    wait_all(stores)


def backward_body(
    x_index,
    own,
    left,
    right,
    far_low,
    far_high,
    to_gate_ref,
    to_up_ref,
    gate_ref,
    up_ref,
    down_ref,
    y_ref,
    z_ref,
    x_ref,
    gate,
    up,
    down,
    y,
    z,
    sems,
    y_sems,
    z_sems,
):
    me = x_index[0]
    whole, low, high = pl.ds(0, 8), pl.ds(0, 4), pl.ds(4, 4)
    pieces = ((own, whole, 0), (left, whole, 3), (right, whole, 1), (far_low, low, 2), (far_high, high, 2))
    loads = [pltpu.make_async_copy(down_ref, down, sems.at[5])]
    for number, (source, planes, away) in enumerate(pieces):
        target = x_ref.at[planes, lax.rem(me + away, 4)]
        loads.append(pltpu.make_async_copy(source, target, sems.at[number]))
    loads.append(pltpu.make_async_copy(gate_ref, gate, sems.at[6]))
    loads.append(pltpu.make_async_copy(up_ref, up, sems.at[7]))
    start_all(loads)
    wait_all(loads[:6])
    x = x_ref[...].reshape(DEPTH, WIDE)
    tail = x[:, MAIN:]
    grad_hidden = f32_dot(down[0], x, NN)
    wait_all(loads[6:])
    tail_hidden, tail_to_gate, tail_to_up = activation(f32_dot(gate[0], tail, NN), f32_dot(up[0], tail, NN))
    tail_grad = grad_hidden[:, MAIN:]
    grad_hidden = grad_hidden[:, :MAIN]
    is_low = lax.broadcasted_iota(jnp.int32, tail_grad.shape, 1) < TAIL
    tail_hidden = jnp.where(is_low, tail_hidden, 0.0).astype(jnp.bfloat16)
    tail_gate = jnp.where(is_low, 0.0, tail_grad * pltpu.roll(tail_to_gate, TAIL, 1)).astype(jnp.bfloat16)
    tail_up = jnp.where(is_low, 0.0, tail_grad * pltpu.roll(tail_to_up, TAIL, 1)).astype(jnp.bfloat16)
    grad_gate = jnp.concatenate([(grad_hidden * to_gate_ref[...]).astype(jnp.bfloat16), tail_gate], axis=1)
    grad_up = jnp.concatenate([(grad_hidden * to_up_ref[...]).astype(jnp.bfloat16), tail_up], axis=1)
    stores = []
    for step in range(PLANES):
        part = pl.ds(step * STEP, STEP)
        value = f32_dot(gate[0, :, part], grad_gate, TN) + f32_dot(up[0, :, part], grad_up, TN)
        out = f32_dot(down[0, :, part], tail_hidden, TN)
        y[step] = value[:, :NEAR].astype(jnp.bfloat16)
        rest = jnp.concatenate([value[:, NEAR:MAIN], value[:, MAIN:] + out], axis=1)
        z[:, step] = rest.astype(jnp.bfloat16).reshape(4, FEATURES, WIDE - NEAR)
        stores.append(pltpu.make_async_copy(y.at[step], y_ref.at[step], y_sems.at[step]))
        stores.append(pltpu.make_async_copy(z.at[:, step], z_ref.at[:, step], z_sems.at[step]))
        start_all(stores[-2:])
    wait_all(stores)


def call(body, outs, *args, specs=None, out_specs=None, scratch=(), limit=24):
    vmem = pl.BlockSpec(memory_space=pltpu.VMEM)
    return pl.pallas_call(
        body,
        out_shape=outs,
        in_specs=specs or [vmem] * len(args),
        out_specs=out_specs or jax.tree.map(lambda _: vmem, outs),
        scratch_shapes=scratch,
        compiler_params=pltpu.CompilerParams(vmem_limit_bytes=limit * 2**20),
    )(*args)


def bf16(*shape):
    return jax.ShapeDtypeStruct(shape, jnp.bfloat16)


def shards(tokens, routes, gate_fixed, gate_weight, up_weight, down_weight, cotangent):
    named = (routes.T, gate_fixed.T)
    weights = (gate_weight, up_weight, down_weight)
    send = call(dispatch_body, bf16(EXPERTS, CAP, 2 * FEATURES), *named, tokens.T, cotangent.T)
    received = lax.all_to_all(send, EP, 0, 0, tiled=True)
    first, second = call(columns_body, (bf16(FEATURES, MAIN), bf16(FEATURES, WIDE)), received)

    first = lax.all_gather(first, "x", axis=0, tiled=True)
    first, second = lax.optimization_barrier((first, second))
    first = lax.all_gather(first, "z", axis=0, tiled=True)
    own = lax.all_gather(second, "z", axis=0, tiled=False)
    left = lax.ppermute(own, "x", RIGHT)
    right = lax.ppermute(own, "x", LEFT)
    first, left, right = lax.optimization_barrier((first, left, right))
    vmem, hbm = pl.BlockSpec(memory_space=pltpu.VMEM), pl.BlockSpec(memory_space=pltpu.HBM)
    weight = pltpu.VMEM(gate_weight.shape, jnp.bfloat16)
    semaphores = pltpu.SemaphoreType.DMA((8,))
    scale = jax.ShapeDtypeStruct((gate_weight.shape[1], MAIN), jnp.float32)
    y_first, to_gate, to_up = call(
        forward_body,
        (bf16(PLANES, STEP, MAIN), scale, scale),
        first,
        *weights,
        specs=[hbm] * 4,
        out_specs=(hbm, vmem, vmem),
        scratch=[pltpu.VMEM((DEPTH, MAIN), jnp.bfloat16)]
        + [weight] * 3
        + [pltpu.VMEM((PLANES, STEP, MAIN), jnp.bfloat16), semaphores, semaphores],
        limit=56,
    )
    left, right, to_gate = lax.optimization_barrier((left, right, to_gate))
    far_low = lax.ppermute(left[:4], "x", RIGHT)
    far_high = lax.ppermute(right[4:], "x", LEFT)
    y_first = lax.psum_scatter(y_first, "z", scatter_dimension=0, tiled=False)
    y_second, y_third = call(
        backward_body,
        (bf16(PLANES, STEP, NEAR), bf16(4, PLANES, FEATURES, WIDE - NEAR)),
        lax.axis_index("x").astype(jnp.int32).reshape(1),
        own,
        left,
        right,
        far_low,
        far_high,
        to_gate,
        to_up,
        *weights,
        specs=[pl.BlockSpec(memory_space=pltpu.SMEM)] + [hbm] * 5 + [vmem] * 2 + [hbm] * 3,
        out_specs=(hbm, hbm),
        scratch=[pltpu.VMEM((PLANES, 4, FEATURES, WIDE), jnp.bfloat16)]
        + [weight] * 3
        + [
            pltpu.VMEM((PLANES, STEP, NEAR), jnp.bfloat16),
            pltpu.VMEM((4, PLANES, FEATURES, WIDE - NEAR), jnp.bfloat16),
            semaphores,
            semaphores,
            semaphores,
        ],
        limit=56,
    )
    y_second = lax.psum_scatter(y_second, "z", scatter_dimension=0, tiled=False)
    y_third = lax.all_to_all(y_third, "x", 0, 0, tiled=True)
    y_third = jnp.sum(y_third.astype(jnp.float32), axis=0).astype(jnp.bfloat16)
    y_third = lax.all_to_all(y_third, "z", 0, 0, tiled=True)
    y_first = lax.all_to_all(y_first.reshape(4, FEATURES, MAIN), "x", 0, 0, tiled=True)
    y_first, y_third, y_second = lax.optimization_barrier((y_first, y_third, y_second))
    y_second = lax.all_to_all(y_second.reshape(4, FEATURES, NEAR), "x", 0, 0, tiled=True)

    back = call(rows_body, bf16(EXPERTS, CAP, 2 * FEATURES), y_first, y_second, y_third)
    home = lax.all_to_all(back, EP, 0, 0, tiled=True)
    out, grad = call(combine_body, (bf16(FEATURES, TOKENS_HERE), bf16(FEATURES, TOKENS_HERE)), *named, home)
    return out.T, grad.T


def solution(mesh):
    fine = Mesh(mesh.devices.reshape(8, 2, 8, 4), ("y", "c", "z", "x"))
    ep, etp = EP, ETP
    placed = (P(ep, etp), P(ep, None), P(ep, None), P(ep, etp, None), P(ep, etp, None), P(ep, etp, None), P(ep, etp))
    return jax.shard_map(shards, mesh=fine, in_specs=placed, out_specs=(P(ep, etp), P(ep, etp)), check_vma=False)
```

```python
import jax
import jax.numpy as jnp
from jax import lax
from jax.experimental import pallas as pl
from jax.experimental.pallas import tpu as pltpu
from jax.sharding import Mesh
from jax.sharding import PartitionSpec as P

EXPERTS = 16
CAP = 36
TOKENS_HERE = 128
FEATURES = 96
ROWS = EXPERTS * CAP
MAIN = 512
TAIL = ROWS - MAIN
WIDE = MAIN + 2 * TAIL
PLANES = 8
STEP = 4 * FEATURES
DEPTH = PLANES * STEP
EP = ("y", "c")
ETP = ("z", "x")
RIGHT = [(0, 1), (1, 2), (2, 3), (3, 0)]
LEFT = [(1, 0), (2, 1), (3, 2), (0, 3)]
NT = (((1,), (1,)), ((), ()))
TN = (((0,), (0,)), ((), ()))
NN = (((1,), (0,)), ((), ()))


def f32_dot(a, b, dims):
    return lax.dot_general(a, b, dims, preferred_element_type=jnp.float32)


def slots(routes, gate_fixed):
    named = []
    gates = []
    for e in range(EXPERTS):
        hit = routes == e
        named.append(jnp.sum(hit.astype(jnp.float32), axis=0, keepdims=True))
        gates.append(jnp.sum(jnp.where(hit, gate_fixed, 0).astype(jnp.float32), axis=0, keepdims=True))
    member = jnp.concatenate(named, axis=0)
    before = lax.broadcasted_iota(jnp.int32, (TOKENS_HERE, TOKENS_HERE), 0)
    after = lax.broadcasted_iota(jnp.int32, (TOKENS_HERE, TOKENS_HERE), 1)
    earlier = (before < after).astype(jnp.bfloat16)
    rank = jnp.dot(member.astype(jnp.bfloat16), earlier, preferred_element_type=jnp.float32)
    rank = jnp.where(member > 0.0, rank, -1.0)
    slot = lax.broadcasted_iota(jnp.int32, (CAP, TOKENS_HERE), 0).astype(jnp.float32)
    onehot = [(rank[e : e + 1] == slot).astype(jnp.float32) for e in range(EXPERTS)]
    return onehot, gates


def dispatch_body(routes_ref, gate_ref, tokens_ref, cot_ref, out_ref):
    onehot, gates = slots(routes_ref[...], gate_ref[...])
    values = jnp.concatenate([tokens_ref[...], cot_ref[...]], axis=0)
    is_token = lax.broadcasted_iota(jnp.int32, (CAP, 2 * FEATURES), 1) < FEATURES
    for e in range(EXPERTS):
        scale = jnp.sum(onehot[e] * gates[e], axis=1, keepdims=True) * (1.0 / 65536.0)
        rows = f32_dot(onehot[e].astype(jnp.bfloat16), values, NT)
        out_ref[e] = (rows * jnp.where(is_token, 1.0, scale)).astype(jnp.bfloat16)


def place_of(source):
    slot = lax.broadcasted_iota(jnp.int32, (CAP, MAIN + 2 * TAIL), 0)
    number = lax.broadcasted_iota(jnp.int32, (CAP, MAIN + 2 * TAIL), 1)
    return (number == slot + source * CAP).astype(jnp.bfloat16)


def columns_body(rows_ref, first_ref, second_ref):
    total = jnp.zeros((2 * FEATURES, WIDE), jnp.float32)
    for source in range(EXPERTS):
        total = total + f32_dot(rows_ref[source], place_of(source), TN)
    tokens, cotangent = total[:FEATURES], total[FEATURES:]
    first_ref[:, pl.ds(0, MAIN)] = tokens[:, :MAIN].astype(jnp.bfloat16)
    low = lax.broadcasted_iota(jnp.int32, (FEATURES, 2 * TAIL), 1) < TAIL
    tail = jnp.where(low, tokens[:, MAIN:], pltpu.roll(cotangent[:, MAIN:], TAIL, 1))
    first_ref[:, pl.ds(MAIN, 2 * TAIL)] = tail.astype(jnp.bfloat16)
    second_ref[...] = cotangent[:, :MAIN].astype(jnp.bfloat16)


def total_of(ref):
    total = ref[0].astype(jnp.float32)
    for k in range(1, ref.shape[0]):
        total = total + ref[k].astype(jnp.float32)
    return total


def rows_body(first_ref, second_ref, out_ref):
    first = total_of(first_ref)
    second = total_of(second_ref)
    tail = second[:, MAIN:]
    low = lax.broadcasted_iota(jnp.int32, tail.shape, 1) < TAIL
    outs = jnp.concatenate([first, jnp.where(low, tail, 0.0)], axis=1)
    grads = jnp.concatenate([second[:, :MAIN], jnp.where(low, pltpu.roll(tail, TAIL, 1), 0.0)], axis=1)
    both = jnp.concatenate([outs, grads], axis=0).astype(jnp.bfloat16)
    for source in range(EXPERTS):
        out_ref[source] = f32_dot(place_of(source), both, NT).astype(jnp.bfloat16)


def combine_body(routes_ref, gate_ref, rows_ref, out_ref, grad_ref):
    onehot, gates = slots(routes_ref[...], gate_ref[...])
    total = jnp.zeros((2 * FEATURES, 3 * TOKENS_HERE), jnp.float32)
    for e in range(EXPERTS):
        high = jnp.floor(gates[e] * (1.0 / 256.0))
        low = gates[e] - 256.0 * high
        factors = jnp.concatenate([onehot[e] * high, onehot[e] * low, onehot[e]], axis=1).astype(jnp.bfloat16)
        total = total + f32_dot(rows_ref[e], factors, TN)
    by_high, by_low = total[:FEATURES, :TOKENS_HERE], total[:FEATURES, TOKENS_HERE : 2 * TOKENS_HERE]
    out_ref[...] = (by_high * (1.0 / 256.0) + by_low * (1.0 / 65536.0)).astype(jnp.bfloat16)
    grad_ref[...] = total[FEATURES:, 2 * TOKENS_HERE :].astype(jnp.bfloat16)


def activation(pre_gate, pre_up):
    sig = jax.nn.sigmoid(pre_gate)
    activated = pre_gate * sig
    derivative = sig * (1.0 + pre_gate * (1.0 - sig))
    return activated * pre_up, pre_up * derivative, activated


def start_all(copies):
    for copy in copies:
        copy.start()


def wait_all(copies):
    for copy in copies:
        copy.wait()


def expert_body(
    x_index,
    first_ref,
    own,
    left,
    right,
    far_low,
    far_high,
    gate_ref,
    up_ref,
    down_ref,
    y_first_ref,
    y_second_ref,
    first,
    second,
    gate,
    up,
    down,
    y_first,
    y_second,
    sems,
    first_sems,
    second_sems,
):
    me = x_index[0]
    whole, low, high = pl.ds(0, 8), pl.ds(0, 4), pl.ds(4, 4)
    pieces = ((own, whole, 0), (left, whole, 3), (right, whole, 1), (far_low, low, 2), (far_high, high, 2))
    loads = [
        pltpu.make_async_copy(source, target, sems.at[number])
        for number, (source, target) in enumerate(((first_ref, first), (gate_ref, gate), (up_ref, up), (down_ref, down)))
    ]
    for number, (source, planes, away) in enumerate(pieces):
        target = second.at[planes, lax.rem(me + away, 4)]
        loads.append(pltpu.make_async_copy(source, target, sems.at[4 + number]))
    start_all(loads)
    wait_all(loads[:2])
    pre_gate = f32_dot(gate[0], first[...], NN)
    loads[2].wait()
    pre_up = f32_dot(up[0], first[...], NN)
    hidden, to_gate, to_up = activation(pre_gate, pre_up)
    wait_all(loads[3:])
    grad_hidden = f32_dot(down[0], second[...].reshape(DEPTH, MAIN), NN)
    tail_grad = f32_dot(down[0], first[:, pl.ds(MAIN, 2 * TAIL)], NN)
    is_low = lax.broadcasted_iota(jnp.int32, tail_grad.shape, 1) < TAIL
    tail_hidden = jnp.where(is_low, hidden[:, MAIN:], 0.0).astype(jnp.bfloat16)
    tail_gate = jnp.where(is_low, 0.0, tail_grad * pltpu.roll(to_gate[:, MAIN:], TAIL, 1)).astype(jnp.bfloat16)
    tail_up = jnp.where(is_low, 0.0, tail_grad * pltpu.roll(to_up[:, MAIN:], TAIL, 1)).astype(jnp.bfloat16)
    grad_gate = jnp.concatenate([(grad_hidden * to_gate[:, :MAIN]).astype(jnp.bfloat16), tail_gate], axis=1)
    grad_up = jnp.concatenate([(grad_hidden * to_up[:, :MAIN]).astype(jnp.bfloat16), tail_up], axis=1)
    hidden = jnp.concatenate([hidden[:, :MAIN].astype(jnp.bfloat16), tail_hidden], axis=1)
    stores = []
    for step in range(PLANES):
        part = pl.ds(step * STEP, STEP)
        out = f32_dot(down[0, :, part], hidden, TN)
        value = f32_dot(gate[0, :, part], grad_gate, TN) + f32_dot(up[0, :, part], grad_up, TN)
        y_first[:, step] = out[:, :MAIN].astype(jnp.bfloat16).reshape(4, FEATURES, MAIN)
        y_second[step, :, pl.ds(0, MAIN)] = value[:, :MAIN].astype(jnp.bfloat16)
        y_second[step, :, pl.ds(MAIN, 2 * TAIL)] = (value[:, MAIN:] + out[:, MAIN:]).astype(jnp.bfloat16)
        stores.append(pltpu.make_async_copy(y_first.at[:, step], y_first_ref.at[:, step], first_sems.at[step]))
        stores.append(pltpu.make_async_copy(y_second.at[step], y_second_ref.at[step], second_sems.at[step]))
        start_all(stores[-2:])
    wait_all(stores)


def call(body, outs, *args, specs=None, out_specs=None, scratch=(), limit=24):
    vmem = pl.BlockSpec(memory_space=pltpu.VMEM)
    return pl.pallas_call(
        body,
        out_shape=outs,
        in_specs=specs or [vmem] * len(args),
        out_specs=out_specs or jax.tree.map(lambda _: vmem, outs),
        scratch_shapes=scratch,
        compiler_params=pltpu.CompilerParams(vmem_limit_bytes=limit * 2**20),
    )(*args)


def bf16(*shape):
    return jax.ShapeDtypeStruct(shape, jnp.bfloat16)


def shards(tokens, routes, gate_fixed, gate_weight, up_weight, down_weight, cotangent):
    named = (routes.T, gate_fixed.T)
    weights = (gate_weight, up_weight, down_weight)
    send = call(dispatch_body, bf16(EXPERTS, CAP, 2 * FEATURES), *named, tokens.T, cotangent.T, limit=56)
    received = lax.all_to_all(send, EP, 0, 0, tiled=True)
    first, second = call(columns_body, (bf16(FEATURES, WIDE), bf16(FEATURES, MAIN)), received)

    first = lax.all_gather(first, "x", axis=0, tiled=True)
    first, second = lax.optimization_barrier((first, second))
    first = lax.all_gather(first, "z", axis=0, tiled=True)
    own = lax.all_gather(second, "z", axis=0, tiled=False)
    left = lax.ppermute(own, "x", RIGHT)
    right = lax.ppermute(own, "x", LEFT)
    far_low = lax.ppermute(left[:4], "x", RIGHT)
    far_high = lax.ppermute(right[4:], "x", LEFT)

    hbm = pl.BlockSpec(memory_space=pltpu.HBM)
    weight = pltpu.VMEM(gate_weight.shape, jnp.bfloat16)
    outs = (bf16(4, PLANES, FEATURES, MAIN), bf16(PLANES, STEP, WIDE))
    y_first, y_second = call(
        expert_body,
        outs,
        lax.axis_index("x").astype(jnp.int32).reshape(1),
        first,
        own,
        left,
        right,
        far_low,
        far_high,
        *weights,
        specs=[pl.BlockSpec(memory_space=pltpu.SMEM)] + [hbm] * 9,
        out_specs=(hbm, hbm),
        scratch=[pltpu.VMEM((DEPTH, WIDE), jnp.bfloat16), pltpu.VMEM((PLANES, 4, FEATURES, MAIN), jnp.bfloat16)]
        + [weight] * 3
        + [pltpu.VMEM(out.shape, jnp.bfloat16) for out in outs]
        + [pltpu.SemaphoreType.DMA((9,)), pltpu.SemaphoreType.DMA((PLANES,)), pltpu.SemaphoreType.DMA((PLANES,))],
        limit=56,
    )
    y_second = lax.psum_scatter(y_second, "z", scatter_dimension=0, tiled=False)
    y_first = lax.all_to_all(y_first, "x", 0, 0, tiled=True)
    y_first = jnp.sum(y_first.astype(jnp.float32), axis=0).astype(jnp.bfloat16)
    y_first = lax.all_to_all(y_first, "z", 0, 0, tiled=True)
    y_first, y_second = lax.optimization_barrier((y_first, y_second))
    y_second = lax.all_to_all(y_second.reshape(4, FEATURES, WIDE), "x", 0, 0, tiled=True)

    back = call(rows_body, bf16(EXPERTS, CAP, 2 * FEATURES), y_first, y_second)
    home = lax.all_to_all(back, EP, 0, 0, tiled=True)
    out, grad = call(combine_body, (bf16(FEATURES, TOKENS_HERE), bf16(FEATURES, TOKENS_HERE)), *named, home)
    return out.T, grad.T


def solution(mesh):
    fine = Mesh(mesh.devices.reshape(8, 2, 8, 4), ("y", "c", "z", "x"))
    ep, etp = EP, ETP
    placed = (P(ep, etp), P(ep, None), P(ep, None), P(ep, etp, None), P(ep, etp, None), P(ep, etp, None), P(ep, etp))
    return jax.shard_map(shards, mesh=fine, in_specs=placed, out_specs=(P(ep, etp), P(ep, etp)), check_vma=False)
```

```python
import jax
import jax.numpy as jnp
from jax import lax
from jax.experimental import pallas as pl
from jax.experimental.pallas import tpu as pltpu
from jax.sharding import Mesh
from jax.sharding import PartitionSpec as P

EXPERTS = 16
CAP = 36
TOKENS_HERE = 128
FEATURES = 96
ROWS = EXPERTS * CAP
MAIN = 512
TAIL = ROWS - MAIN
WIDE = MAIN + 2 * TAIL
PLANES = 8
STEP = 4 * FEATURES
DEPTH = PLANES * STEP
EP = ("y", "c")
ETP = ("z", "x")
RIGHT = [(0, 1), (1, 2), (2, 3), (3, 0)]
LEFT = [(1, 0), (2, 1), (3, 2), (0, 3)]
NT = (((1,), (1,)), ((), ()))
TN = (((0,), (0,)), ((), ()))
NN = (((1,), (0,)), ((), ()))


def f32_dot(a, b, dims):
    return lax.dot_general(a, b, dims, preferred_element_type=jnp.float32)


def slots(routes, gate_fixed):
    named = []
    gates = []
    for e in range(EXPERTS):
        hit = routes == e
        named.append(jnp.sum(hit.astype(jnp.float32), axis=0, keepdims=True))
        gates.append(jnp.sum(jnp.where(hit, gate_fixed, 0).astype(jnp.float32), axis=0, keepdims=True))
    member = jnp.concatenate(named, axis=0)
    before = lax.broadcasted_iota(jnp.int32, (TOKENS_HERE, TOKENS_HERE), 0)
    after = lax.broadcasted_iota(jnp.int32, (TOKENS_HERE, TOKENS_HERE), 1)
    earlier = (before < after).astype(jnp.bfloat16)
    rank = jnp.dot(member.astype(jnp.bfloat16), earlier, preferred_element_type=jnp.float32)
    rank = jnp.where(member > 0.0, rank, -1.0)
    slot = lax.broadcasted_iota(jnp.int32, (CAP, TOKENS_HERE), 0).astype(jnp.float32)
    onehot = [(rank[e : e + 1] == slot).astype(jnp.float32) for e in range(EXPERTS)]
    return onehot, gates


def dispatch_body(routes_ref, gate_ref, tokens_ref, cot_ref, out_ref):
    onehot, gates = slots(routes_ref[...], gate_ref[...])
    values = jnp.concatenate([tokens_ref[...], cot_ref[...]], axis=0)
    is_token = lax.broadcasted_iota(jnp.int32, (CAP, 2 * FEATURES), 1) < FEATURES
    for e in range(EXPERTS):
        scale = jnp.sum(onehot[e] * gates[e], axis=1, keepdims=True) * (1.0 / 65536.0)
        rows = f32_dot(onehot[e].astype(jnp.bfloat16), values, NT)
        out_ref[e] = (rows * jnp.where(is_token, 1.0, scale)).astype(jnp.bfloat16)


def place_of(source):
    slot = lax.broadcasted_iota(jnp.int32, (CAP, MAIN + 2 * TAIL), 0)
    number = lax.broadcasted_iota(jnp.int32, (CAP, MAIN + 2 * TAIL), 1)
    return (number == slot + source * CAP).astype(jnp.bfloat16)


def columns_body(rows_ref, first_ref, second_ref):
    total = jnp.zeros((2 * FEATURES, WIDE), jnp.float32)
    for source in range(EXPERTS):
        total = total + f32_dot(rows_ref[source], place_of(source), TN)
    tokens, cotangent = total[:FEATURES], total[FEATURES:]
    first_ref[:, pl.ds(0, MAIN)] = tokens[:, :MAIN].astype(jnp.bfloat16)
    low = lax.broadcasted_iota(jnp.int32, (FEATURES, 2 * TAIL), 1) < TAIL
    tail = jnp.where(low, tokens[:, MAIN:], pltpu.roll(cotangent[:, MAIN:], TAIL, 1))
    first_ref[:, pl.ds(MAIN, 2 * TAIL)] = tail.astype(jnp.bfloat16)
    second_ref[...] = cotangent[:, :MAIN].astype(jnp.bfloat16)


def total_of(ref):
    total = ref[0].astype(jnp.float32)
    for k in range(1, ref.shape[0]):
        total = total + ref[k].astype(jnp.float32)
    return total


def rows_body(first_ref, second_ref, out_ref):
    first = total_of(first_ref)
    second = total_of(second_ref)
    tail = second[:, MAIN:]
    low = lax.broadcasted_iota(jnp.int32, tail.shape, 1) < TAIL
    outs = jnp.concatenate([first, jnp.where(low, tail, 0.0)], axis=1)
    grads = jnp.concatenate([second[:, :MAIN], jnp.where(low, pltpu.roll(tail, TAIL, 1), 0.0)], axis=1)
    both = jnp.concatenate([outs, grads], axis=0).astype(jnp.bfloat16)
    for source in range(EXPERTS):
        out_ref[source] = f32_dot(place_of(source), both, NT).astype(jnp.bfloat16)


def combine_body(routes_ref, gate_ref, rows_ref, out_ref, grad_ref):
    onehot, gates = slots(routes_ref[...], gate_ref[...])
    total = jnp.zeros((2 * FEATURES, 3 * TOKENS_HERE), jnp.float32)
    for e in range(EXPERTS):
        high = jnp.floor(gates[e] * (1.0 / 256.0))
        low = gates[e] - 256.0 * high
        factors = jnp.concatenate([onehot[e] * high, onehot[e] * low, onehot[e]], axis=1).astype(jnp.bfloat16)
        total = total + f32_dot(rows_ref[e], factors, TN)
    by_high, by_low = total[:FEATURES, :TOKENS_HERE], total[:FEATURES, TOKENS_HERE : 2 * TOKENS_HERE]
    out_ref[...] = (by_high * (1.0 / 256.0) + by_low * (1.0 / 65536.0)).astype(jnp.bfloat16)
    grad_ref[...] = total[FEATURES:, 2 * TOKENS_HERE :].astype(jnp.bfloat16)


def activation(pre_gate, pre_up):
    sig = jax.nn.sigmoid(pre_gate)
    activated = pre_gate * sig
    derivative = sig * (1.0 + pre_gate * (1.0 - sig))
    return activated * pre_up, pre_up * derivative, activated


def start_all(copies):
    for copy in copies:
        copy.start()


def wait_all(copies):
    for copy in copies:
        copy.wait()


def expert_body(
    x_index,
    first_ref,
    own,
    left_low,
    left_high,
    right_low,
    right_high,
    far_low,
    far_high,
    gate_ref,
    up_ref,
    down_ref,
    y_first_ref,
    y_second_ref,
    first,
    second,
    gate,
    up,
    down,
    y_first,
    y_second,
    sems,
    first_sems,
    second_sems,
):
    me = x_index[0]
    whole, low, high = pl.ds(0, 8), pl.ds(0, 4), pl.ds(4, 4)
    pieces = (
        (own, whole, 0),
        (left_low, low, 3),
        (left_high, high, 3),
        (right_low, low, 1),
        (right_high, high, 1),
        (far_low, low, 2),
        (far_high, high, 2),
    )
    loads = [
        pltpu.make_async_copy(source, target, sems.at[number])
        for number, (source, target) in enumerate(((first_ref, first), (gate_ref, gate), (up_ref, up), (down_ref, down)))
    ]
    for number, (source, planes, away) in enumerate(pieces):
        target = second.at[planes, lax.rem(me + away, 4)]
        loads.append(pltpu.make_async_copy(source, target, sems.at[4 + number]))
    start_all(loads)
    wait_all(loads[:2])
    pre_gate = f32_dot(gate[0], first[...], NN)
    loads[2].wait()
    pre_up = f32_dot(up[0], first[...], NN)
    hidden, to_gate, to_up = activation(pre_gate, pre_up)
    wait_all(loads[3:])
    grad_hidden = f32_dot(down[0], second[...].reshape(DEPTH, MAIN), NN)
    tail_grad = f32_dot(down[0], first[:, pl.ds(MAIN, 2 * TAIL)], NN)
    is_low = lax.broadcasted_iota(jnp.int32, tail_grad.shape, 1) < TAIL
    tail_hidden = jnp.where(is_low, hidden[:, MAIN:], 0.0).astype(jnp.bfloat16)
    tail_gate = jnp.where(is_low, 0.0, tail_grad * pltpu.roll(to_gate[:, MAIN:], TAIL, 1)).astype(jnp.bfloat16)
    tail_up = jnp.where(is_low, 0.0, tail_grad * pltpu.roll(to_up[:, MAIN:], TAIL, 1)).astype(jnp.bfloat16)
    grad_gate = jnp.concatenate([(grad_hidden * to_gate[:, :MAIN]).astype(jnp.bfloat16), tail_gate], axis=1)
    grad_up = jnp.concatenate([(grad_hidden * to_up[:, :MAIN]).astype(jnp.bfloat16), tail_up], axis=1)
    hidden = jnp.concatenate([hidden[:, :MAIN].astype(jnp.bfloat16), tail_hidden], axis=1)
    stores = []
    for step in range(PLANES):
        part = pl.ds(step * STEP, STEP)
        out = f32_dot(down[0, :, part], hidden, TN)
        value = f32_dot(gate[0, :, part], grad_gate, TN) + f32_dot(up[0, :, part], grad_up, TN)
        y_first[:, step] = out[:, :MAIN].astype(jnp.bfloat16).reshape(4, FEATURES, MAIN)
        y_second[step, :, pl.ds(0, MAIN)] = value[:, :MAIN].astype(jnp.bfloat16)
        y_second[step, :, pl.ds(MAIN, 2 * TAIL)] = (value[:, MAIN:] + out[:, MAIN:]).astype(jnp.bfloat16)
        stores.append(pltpu.make_async_copy(y_first.at[:, step], y_first_ref.at[:, step], first_sems.at[step]))
        stores.append(pltpu.make_async_copy(y_second.at[step], y_second_ref.at[step], second_sems.at[step]))
        start_all(stores[-2:])
    wait_all(stores)


def call(body, outs, *args, specs=None, out_specs=None, scratch=(), limit=24):
    vmem = pl.BlockSpec(memory_space=pltpu.VMEM)
    return pl.pallas_call(
        body,
        out_shape=outs,
        in_specs=specs or [vmem] * len(args),
        out_specs=out_specs or jax.tree.map(lambda _: vmem, outs),
        scratch_shapes=scratch,
        compiler_params=pltpu.CompilerParams(vmem_limit_bytes=limit * 2**20),
    )(*args)


def bf16(*shape):
    return jax.ShapeDtypeStruct(shape, jnp.bfloat16)


def shards(tokens, routes, gate_fixed, gate_weight, up_weight, down_weight, cotangent):
    named = (routes.T, gate_fixed.T)
    weights = (gate_weight, up_weight, down_weight)
    send = call(dispatch_body, bf16(EXPERTS, CAP, 2 * FEATURES), *named, tokens.T, cotangent.T, limit=56)
    received = lax.all_to_all(send, EP, 0, 0, tiled=True)
    first, second = call(columns_body, (bf16(FEATURES, WIDE), bf16(FEATURES, MAIN)), received)

    first = lax.all_gather(first, "x", axis=0, tiled=True)
    first, second = lax.optimization_barrier((first, second))
    first = lax.all_gather(first, "z", axis=0, tiled=True)
    own = lax.all_gather(second, "z", axis=0, tiled=False)
    left_low = lax.ppermute(own[:4], "x", RIGHT)
    right_high = lax.ppermute(own[4:], "x", LEFT)
    left_high = lax.ppermute(own[4:], "x", RIGHT)
    right_low = lax.ppermute(own[:4], "x", LEFT)
    far_low = lax.ppermute(left_low, "x", RIGHT)
    far_high = lax.ppermute(right_high, "x", LEFT)

    hbm = pl.BlockSpec(memory_space=pltpu.HBM)
    weight = pltpu.VMEM(gate_weight.shape, jnp.bfloat16)
    outs = (bf16(4, PLANES, FEATURES, MAIN), bf16(PLANES, STEP, WIDE))
    y_first, y_second = call(
        expert_body,
        outs,
        lax.axis_index("x").astype(jnp.int32).reshape(1),
        first,
        own,
        left_low,
        left_high,
        right_low,
        right_high,
        far_low,
        far_high,
        *weights,
        specs=[pl.BlockSpec(memory_space=pltpu.SMEM)] + [hbm] * 11,
        out_specs=(hbm, hbm),
        scratch=[pltpu.VMEM((DEPTH, WIDE), jnp.bfloat16), pltpu.VMEM((PLANES, 4, FEATURES, MAIN), jnp.bfloat16)]
        + [weight] * 3
        + [pltpu.VMEM(out.shape, jnp.bfloat16) for out in outs]
        + [pltpu.SemaphoreType.DMA((11,)), pltpu.SemaphoreType.DMA((PLANES,)), pltpu.SemaphoreType.DMA((PLANES,))],
        limit=56,
    )
    y_second = lax.psum_scatter(y_second, "z", scatter_dimension=0, tiled=False)
    y_first = lax.all_to_all(y_first, "x", 0, 0, tiled=True)
    y_first = jnp.sum(y_first.astype(jnp.float32), axis=0).astype(jnp.bfloat16)
    y_first = lax.all_to_all(y_first, "z", 0, 0, tiled=True)
    y_first, y_second = lax.optimization_barrier((y_first, y_second))
    y_second = lax.all_to_all(y_second.reshape(4, FEATURES, WIDE), "x", 0, 0, tiled=True)

    back = call(rows_body, bf16(EXPERTS, CAP, 2 * FEATURES), y_first, y_second)
    home = lax.all_to_all(back, EP, 0, 0, tiled=True)
    out, grad = call(combine_body, (bf16(FEATURES, TOKENS_HERE), bf16(FEATURES, TOKENS_HERE)), *named, home)
    return out.T, grad.T


def solution(mesh):
    fine = Mesh(mesh.devices.reshape(8, 2, 8, 4), ("y", "c", "z", "x"))
    ep, etp = EP, ETP
    placed = (P(ep, etp), P(ep, None), P(ep, None), P(ep, etp, None), P(ep, etp, None), P(ep, etp, None), P(ep, etp))
    return jax.shard_map(shards, mesh=fine, in_specs=placed, out_specs=(P(ep, etp), P(ep, etp)), check_vma=False)
```

```python
import jax
import jax.numpy as jnp
from jax import lax
from jax.experimental import pallas as pl
from jax.experimental.pallas import tpu as pltpu
from jax.sharding import Mesh
from jax.sharding import PartitionSpec as P

EXPERTS = 16
CAP = 36
TOKENS_HERE = 128
FEATURES = 96
ROWS = EXPERTS * CAP
MAIN = 512
TAIL = ROWS - MAIN
WIDE = MAIN + 2 * TAIL
PLANES = 8
STEP = 4 * FEATURES
DEPTH = PLANES * STEP
EP = ("y", "c")
ETP = ("z", "x")
RIGHT = [(0, 1), (1, 2), (2, 3), (3, 0)]
LEFT = [(1, 0), (2, 1), (3, 2), (0, 3)]
NT = (((1,), (1,)), ((), ()))
TN = (((0,), (0,)), ((), ()))
NN = (((1,), (0,)), ((), ()))


def f32_dot(a, b, dims):
    return lax.dot_general(a, b, dims, preferred_element_type=jnp.float32)


def slots(routes, gate_fixed):
    named = []
    gates = []
    for e in range(EXPERTS):
        hit = routes == e
        named.append(jnp.sum(hit.astype(jnp.float32), axis=0, keepdims=True))
        gates.append(jnp.sum(jnp.where(hit, gate_fixed, 0).astype(jnp.float32), axis=0, keepdims=True))
    member = jnp.concatenate(named, axis=0)
    before = lax.broadcasted_iota(jnp.int32, (TOKENS_HERE, TOKENS_HERE), 0)
    after = lax.broadcasted_iota(jnp.int32, (TOKENS_HERE, TOKENS_HERE), 1)
    earlier = (before < after).astype(jnp.bfloat16)
    rank = jnp.dot(member.astype(jnp.bfloat16), earlier, preferred_element_type=jnp.float32)
    rank = jnp.where(member > 0.0, rank, -1.0)
    slot = lax.broadcasted_iota(jnp.int32, (CAP, TOKENS_HERE), 0).astype(jnp.float32)
    onehot = [(rank[e : e + 1] == slot).astype(jnp.float32) for e in range(EXPERTS)]
    return onehot, gates


def dispatch_body(routes_ref, gate_ref, tokens_ref, cot_ref, out_ref):
    onehot, gates = slots(routes_ref[...], gate_ref[...])
    values = jnp.concatenate([tokens_ref[...], cot_ref[...]], axis=0)
    is_token = lax.broadcasted_iota(jnp.int32, (CAP, 2 * FEATURES), 1) < FEATURES
    for e in range(EXPERTS):
        scale = jnp.sum(onehot[e] * gates[e], axis=1, keepdims=True) * (1.0 / 65536.0)
        rows = f32_dot(onehot[e].astype(jnp.bfloat16), values, NT)
        out_ref[e] = (rows * jnp.where(is_token, 1.0, scale)).astype(jnp.bfloat16)


def place_of(source):
    slot = lax.broadcasted_iota(jnp.int32, (CAP, MAIN + 2 * TAIL), 0)
    number = lax.broadcasted_iota(jnp.int32, (CAP, MAIN + 2 * TAIL), 1)
    return (number == slot + source * CAP).astype(jnp.bfloat16)


def columns_body(rows_ref, first_ref, second_ref):
    total = jnp.zeros((2 * FEATURES, WIDE), jnp.float32)
    for source in range(EXPERTS):
        total = total + f32_dot(rows_ref[source], place_of(source), TN)
    tokens, cotangent = total[:FEATURES], total[FEATURES:]
    first_ref[:, pl.ds(0, MAIN)] = tokens[:, :MAIN].astype(jnp.bfloat16)
    low = lax.broadcasted_iota(jnp.int32, (FEATURES, 2 * TAIL), 1) < TAIL
    tail = jnp.where(low, tokens[:, MAIN:], pltpu.roll(cotangent[:, MAIN:], TAIL, 1))
    first_ref[:, pl.ds(MAIN, 2 * TAIL)] = tail.astype(jnp.bfloat16)
    second_ref[...] = cotangent[:, :MAIN].astype(jnp.bfloat16)


def total_of(ref):
    total = ref[0].astype(jnp.float32)
    for k in range(1, ref.shape[0]):
        total = total + ref[k].astype(jnp.float32)
    return total


def rows_body(first_ref, second_ref, out_ref):
    first = total_of(first_ref)
    second = total_of(second_ref)
    tail = second[:, MAIN:]
    low = lax.broadcasted_iota(jnp.int32, tail.shape, 1) < TAIL
    outs = jnp.concatenate([first, jnp.where(low, tail, 0.0)], axis=1)
    grads = jnp.concatenate([second[:, :MAIN], jnp.where(low, pltpu.roll(tail, TAIL, 1), 0.0)], axis=1)
    both = jnp.concatenate([outs, grads], axis=0).astype(jnp.bfloat16)
    for source in range(EXPERTS):
        out_ref[source] = f32_dot(place_of(source), both, NT).astype(jnp.bfloat16)


def combine_body(routes_ref, gate_ref, rows_ref, out_ref, grad_ref):
    onehot, gates = slots(routes_ref[...], gate_ref[...])
    total = jnp.zeros((2 * FEATURES, 3 * TOKENS_HERE), jnp.float32)
    for e in range(EXPERTS):
        high = jnp.floor(gates[e] * (1.0 / 256.0))
        low = gates[e] - 256.0 * high
        factors = jnp.concatenate([onehot[e] * high, onehot[e] * low, onehot[e]], axis=1).astype(jnp.bfloat16)
        total = total + f32_dot(rows_ref[e], factors, TN)
    by_high, by_low = total[:FEATURES, :TOKENS_HERE], total[:FEATURES, TOKENS_HERE : 2 * TOKENS_HERE]
    out_ref[...] = (by_high * (1.0 / 256.0) + by_low * (1.0 / 65536.0)).astype(jnp.bfloat16)
    grad_ref[...] = total[FEATURES:, 2 * TOKENS_HERE :].astype(jnp.bfloat16)


def activation(pre_gate, pre_up):
    sig = jax.nn.sigmoid(pre_gate)
    activated = pre_gate * sig
    derivative = sig * (1.0 + pre_gate * (1.0 - sig))
    return activated * pre_up, pre_up * derivative, activated


def start_all(copies):
    for copy in copies:
        copy.start()


def wait_all(copies):
    for copy in copies:
        copy.wait()


def expert_body(
    x_index,
    first_ref,
    own,
    left_low,
    left_high,
    right_low,
    right_high,
    far_low,
    far_high,
    gate_ref,
    up_ref,
    down_ref,
    y_first_ref,
    y_second_ref,
    first,
    second,
    gate,
    up,
    down,
    y_first,
    y_second,
    sems,
    first_sems,
    second_sems,
):
    me = x_index[0]
    whole, low, high = pl.ds(0, 8), pl.ds(0, 4), pl.ds(4, 4)
    pieces = (
        (own, whole, 0),
        (left_low, low, 3),
        (left_high, high, 3),
        (right_low, low, 1),
        (right_high, high, 1),
        (far_low, low, 2),
        (far_high, high, 2),
    )
    loads = [
        pltpu.make_async_copy(source, target, sems.at[number])
        for number, (source, target) in enumerate(((first_ref, first), (gate_ref, gate), (up_ref, up), (down_ref, down)))
    ]
    for number, (source, planes, away) in enumerate(pieces):
        target = second.at[planes, lax.rem(me + away, 4)]
        loads.append(pltpu.make_async_copy(source, target, sems.at[4 + number]))
    start_all(loads[:3])
    wait_all(loads[:2])
    start_all(loads[3:])
    pre_gate = f32_dot(gate[0], first[...], NN)
    loads[2].wait()
    pre_up = f32_dot(up[0], first[...], NN)
    hidden, to_gate, to_up = activation(pre_gate, pre_up)
    wait_all(loads[3:])
    grad_hidden = f32_dot(down[0], second[...].reshape(DEPTH, MAIN), NN)
    tail_grad = f32_dot(down[0], first[:, pl.ds(MAIN, 2 * TAIL)], NN)
    is_low = lax.broadcasted_iota(jnp.int32, tail_grad.shape, 1) < TAIL
    tail_hidden = jnp.where(is_low, hidden[:, MAIN:], 0.0).astype(jnp.bfloat16)
    tail_gate = jnp.where(is_low, 0.0, tail_grad * pltpu.roll(to_gate[:, MAIN:], TAIL, 1)).astype(jnp.bfloat16)
    tail_up = jnp.where(is_low, 0.0, tail_grad * pltpu.roll(to_up[:, MAIN:], TAIL, 1)).astype(jnp.bfloat16)
    grad_gate = jnp.concatenate([(grad_hidden * to_gate[:, :MAIN]).astype(jnp.bfloat16), tail_gate], axis=1)
    grad_up = jnp.concatenate([(grad_hidden * to_up[:, :MAIN]).astype(jnp.bfloat16), tail_up], axis=1)
    hidden = jnp.concatenate([hidden[:, :MAIN].astype(jnp.bfloat16), tail_hidden], axis=1)
    stores = []
    for step in range(PLANES):
        part = pl.ds(step * STEP, STEP)
        out = f32_dot(down[0, :, part], hidden, TN)
        value = f32_dot(gate[0, :, part], grad_gate, TN) + f32_dot(up[0, :, part], grad_up, TN)
        y_first[:, step] = out[:, :MAIN].astype(jnp.bfloat16).reshape(4, FEATURES, MAIN)
        y_second[step, :, pl.ds(0, MAIN)] = value[:, :MAIN].astype(jnp.bfloat16)
        y_second[step, :, pl.ds(MAIN, 2 * TAIL)] = (value[:, MAIN:] + out[:, MAIN:]).astype(jnp.bfloat16)
        stores.append(pltpu.make_async_copy(y_first.at[:, step], y_first_ref.at[:, step], first_sems.at[step]))
        stores.append(pltpu.make_async_copy(y_second.at[step], y_second_ref.at[step], second_sems.at[step]))
        start_all(stores[-2:])
    wait_all(stores)


def call(body, outs, *args, specs=None, out_specs=None, scratch=(), limit=24):
    vmem = pl.BlockSpec(memory_space=pltpu.VMEM)
    return pl.pallas_call(
        body,
        out_shape=outs,
        in_specs=specs or [vmem] * len(args),
        out_specs=out_specs or jax.tree.map(lambda _: vmem, outs),
        scratch_shapes=scratch,
        compiler_params=pltpu.CompilerParams(vmem_limit_bytes=limit * 2**20),
    )(*args)


def bf16(*shape):
    return jax.ShapeDtypeStruct(shape, jnp.bfloat16)


def shards(tokens, routes, gate_fixed, gate_weight, up_weight, down_weight, cotangent):
    named = (routes.T, gate_fixed.T)
    weights = (gate_weight, up_weight, down_weight)
    send = call(dispatch_body, bf16(EXPERTS, CAP, 2 * FEATURES), *named, tokens.T, cotangent.T, limit=56)
    received = lax.all_to_all(send, EP, 0, 0, tiled=True)
    first, second = call(columns_body, (bf16(FEATURES, WIDE), bf16(FEATURES, MAIN)), received)

    first = lax.all_gather(first, "x", axis=0, tiled=True)
    first, second = lax.optimization_barrier((first, second))
    first = lax.all_gather(first, "z", axis=0, tiled=True)
    own = lax.all_gather(second, "z", axis=0, tiled=False)
    left_low = lax.ppermute(own[:4], "x", RIGHT)
    right_high = lax.ppermute(own[4:], "x", LEFT)
    left_high = lax.ppermute(own[4:], "x", RIGHT)
    right_low = lax.ppermute(own[:4], "x", LEFT)
    far_low = lax.ppermute(left_low, "x", RIGHT)
    far_high = lax.ppermute(right_high, "x", LEFT)

    hbm = pl.BlockSpec(memory_space=pltpu.HBM)
    weight = pltpu.VMEM(gate_weight.shape, jnp.bfloat16)
    outs = (bf16(4, PLANES, FEATURES, MAIN), bf16(PLANES, STEP, WIDE))
    y_first, y_second = call(
        expert_body,
        outs,
        lax.axis_index("x").astype(jnp.int32).reshape(1),
        first,
        own,
        left_low,
        left_high,
        right_low,
        right_high,
        far_low,
        far_high,
        *weights,
        specs=[pl.BlockSpec(memory_space=pltpu.SMEM)] + [hbm] * 11,
        out_specs=(hbm, hbm),
        scratch=[pltpu.VMEM((DEPTH, WIDE), jnp.bfloat16), pltpu.VMEM((PLANES, 4, FEATURES, MAIN), jnp.bfloat16)]
        + [weight] * 3
        + [pltpu.VMEM(out.shape, jnp.bfloat16) for out in outs]
        + [pltpu.SemaphoreType.DMA((11,)), pltpu.SemaphoreType.DMA((PLANES,)), pltpu.SemaphoreType.DMA((PLANES,))],
        limit=56,
    )
    y_second = lax.psum_scatter(y_second, "z", scatter_dimension=0, tiled=False)
    y_first = lax.all_to_all(y_first, "x", 0, 0, tiled=True)
    y_first = jnp.sum(y_first.astype(jnp.float32), axis=0).astype(jnp.bfloat16)
    y_first = lax.all_to_all(y_first, "z", 0, 0, tiled=True)
    y_first, y_second = lax.optimization_barrier((y_first, y_second))
    y_second = lax.all_to_all(y_second.reshape(4, FEATURES, WIDE), "x", 0, 0, tiled=True)

    back = call(rows_body, bf16(EXPERTS, CAP, 2 * FEATURES), y_first, y_second)
    home = lax.all_to_all(back, EP, 0, 0, tiled=True)
    out, grad = call(combine_body, (bf16(FEATURES, TOKENS_HERE), bf16(FEATURES, TOKENS_HERE)), *named, home)
    return out.T, grad.T


def solution(mesh):
    fine = Mesh(mesh.devices.reshape(8, 2, 8, 4), ("y", "c", "z", "x"))
    ep, etp = EP, ETP
    placed = (P(ep, etp), P(ep, None), P(ep, None), P(ep, etp, None), P(ep, etp, None), P(ep, etp, None), P(ep, etp))
    return jax.shard_map(shards, mesh=fine, in_specs=placed, out_specs=(P(ep, etp), P(ep, etp)), check_vma=False)
```
